32 devices in a mesh: groups: 2 (over x), cells: 16 (over z, y, core).
Axes of the slice: x: 2, y: 2, z: 4, core: 2. Of those that a mesh axis runs over, the one named last changes fastest.
Arguments:
- features: bfloat16 [12288, 384], P(('groups', 'cells')), parts along dimension 0, may hold values from -40 to 40
- cotangent: bfloat16 [12288, 384], P(('groups', 'cells')), parts along dimension 0, may hold values from -6 to 6
- inner_weight: bfloat16 [384, 1152], replicated, may hold values from -0.3125 to 0.3125
- outer_weight: bfloat16 [384, 384], replicated, may hold values from -0.3125 to 0.3125
- upward_weight: bfloat16 [384, 1536], replicated, may hold values from -0.3125 to 0.3125
- downward_weight: bfloat16 [1536, 384], replicated, may hold values from -0.15625 to 0.15625
- node_mask: int32 [96, 128], P(('groups', 'cells')), parts along dimension 0, may hold values from 0 to 1, as said below
- neighbours: int32 [96, 8], P(('groups', 'cells')), parts along dimension 0, may hold values from 0 to 47, as said below
Outputs:
- back_features: bfloat16 [12288, 384], P(('groups', 'cells')), parts along dimension 0
- grad_inner: float32 [768, 1152], P(('groups', 'cells')), parts along dimension 0
- grad_outer: float32 [768, 384], P(('groups', 'cells')), parts along dimension 0
- grad_up: float32 [768, 1536], P(('groups', 'cells')), parts along dimension 0
- grad_down: float32 [3072, 384], P(('groups', 'cells')), parts along dimension 0
The draws below stay inside these ranges and needn't reach their ends.
There are 2 independent parts, one for each index of `groups`. The reference program is written for one: setup_inputs(seed, part) draws one part's arguments, and reference() takes and returns one part's arrays. A program takes and returns all parts, laid end to end along the dimension named above; an argument that names none is the same for every part. Nothing has to cross between parts.
Inputs may be any that keep to these rules, and one draw needn't show every extreme that they name: `node_mask`: patch slot s of cell c (global id c * 3 + s) is live where s is below the cell's live count, which is 1 to 3, and 3 in the last cell ; empty slots hold only zeros, and the first node of every live patch is 1. `neighbours`: every id names a live patch of a cell at most 2 cells from the patch's own. Slot 0 names the patch itself where it is live, else slot 0 of its cell; slots 1, 2, 3, 4 name patches of the cells at offsets +1, -1, +2, -2, clipped to the first and last cell.
All inputs are finite; a program needn't handle non-finite values.
Results may differ from the reference program's by a relative error of at most 0.017.
Values may be sent and summed in bfloat16 or wider, within the bound.
A program may use at most 128 MiB of HBM per device.

```python
import math
import jax
import jax.numpy as jnp
from jax import lax

D = 384
HEADS = 8
FF = 1536
PATCH_NODES = 128
NEAR = 8
PATCH_DEV = 3
PATCHES = 48
NODES = 6144


def live_counts(key):
    cells = PATCHES // PATCH_DEV
    counts = jax.random.randint(jax.random.fold_in(key, 11), (cells,), 1, PATCH_DEV + 1)
    chosen = jax.random.randint(jax.random.fold_in(key, 12), (), 0, cells)
    spots = jnp.arange(cells)
    return jnp.where((spots == chosen) | (spots == cells - 1), PATCH_DEV, counts)


def draw_node_mask(key, part):
    counts = live_counts(key)
    cell_of = jnp.arange(PATCHES) // PATCH_DEV
    slot_of = jnp.arange(PATCHES) % PATCH_DEV
    live = slot_of < counts[cell_of]
    kept = jax.random.randint(jax.random.fold_in(key, 13), (PATCHES, PATCH_NODES), 0, 5) > 0
    first = jnp.arange(PATCH_NODES)[None, :] == 0
    return (live[:, None] & (kept | first)).astype(jnp.int32)


def draw_neighbours(key, part):
    cells = PATCHES // PATCH_DEV
    counts = live_counts(key)
    cell_of = jnp.arange(PATCHES) // PATCH_DEV
    slot_of = jnp.arange(PATCHES) % PATCH_DEV
    fixed_offsets = jnp.array([0, 1, -1, 2, -2, 0, 0, 0], jnp.int32)
    drawn = jax.random.randint(jax.random.fold_in(key, 14), (PATCHES, NEAR), -2, 3)
    column = jnp.arange(NEAR)[None, :]
    offsets = jnp.where(column < 5, fixed_offsets[None, :], drawn)
    target = jnp.clip(cell_of[:, None] + offsets, 0, cells - 1)
    picked = jax.random.randint(jax.random.fold_in(key, 15), (PATCHES, NEAR), 0, counts[target])
    own_slot = jnp.where(slot_of < counts[cell_of], slot_of, 0)
    chosen_slot = jnp.where(column == 0, own_slot[:, None], picked)
    return (target * PATCH_DEV + chosen_slot).astype(jnp.int32)


def draw_features(key, part):
    base = jax.random.normal(jax.random.fold_in(key, 21), (NODES, D))
    spread = jnp.exp(jax.random.uniform(jax.random.fold_in(key, 22), (NODES, 1)) * math.log(10.0))
    return jnp.clip(base * spread, -40.0, 40.0).astype(jnp.bfloat16)


def levels(key, extent, shards, low, high):
    loudness = 1.0
    for position, blocks in shards:
        steps = jax.random.uniform(jax.random.fold_in(jax.random.fold_in(key, 6), position), (blocks,), jnp.float32, low / len(shards), high / len(shards))
        loudness = loudness * jnp.repeat(jnp.exp(steps), extent[position] // blocks).reshape((-1,) + (1,) * (len(extent) - 1 - position))
    return loudness


def centred(key, shape, scale, reach, cuts=(), kind=jnp.bfloat16):
    values = scale * jax.random.normal(key, shape, jnp.float32)
    if cuts:
        values = values * levels(key, shape, cuts, -0.22, 0.18)
    return jnp.clip(values, -reach, reach).astype(kind)


def setup_inputs(seed: int = 0, part: int = 0) -> dict:
    key_of = jax.random.split(jax.random.key(seed), 9)
    part_splits = jax.random.split(jax.random.fold_in(key_of[8], part), 9)
    return {
        "features": draw_features(jax.random.fold_in(jax.random.fold_in(key_of[8], part), 71), part),
        "cotangent": centred(part_splits[1], (NODES, D), 1.0, 6.0, ((0, 16),)),
        "inner_weight": centred(key_of[2], (D, 3 * D), D ** -0.5, 0.3125),
        "outer_weight": centred(key_of[3], (D, D), D ** -0.5, 0.3125),
        "upward_weight": centred(key_of[4], (D, FF), D ** -0.5, 0.3125),
        "downward_weight": centred(key_of[5], (FF, D), FF ** -0.5, 0.15625),
        "node_mask": draw_node_mask(jax.random.fold_in(jax.random.fold_in(key_of[8], part), 71), part),
        "neighbours": draw_neighbours(jax.random.fold_in(jax.random.fold_in(key_of[8], part), 71), part),
    }


epsilon = 1e-06
score_scale = 5.0
block_patches = 3

def rms_rows(rows):
    return rows * lax.rsqrt(lax.optimization_barrier(jnp.mean(rows * rows, axis=-1, keepdims=True)) + epsilon)

def head_norm(rows):
    count = rows.shape[0]
    split = rows.reshape(count, HEADS, D // HEADS)
    split = split * lax.rsqrt(lax.optimization_barrier(jnp.mean(split * split, axis=-1, keepdims=True)) + epsilon)
    return split.reshape(count, D)

def widen(array):
    return lax.optimization_barrier(array).astype(jnp.float32)

def gather_tiles(index_block, tiles):
    picked = jnp.take(tiles, index_block.reshape(-1), axis=0)
    return picked.reshape(index_block.shape[0], NEAR * PATCH_NODES, HEADS, D // HEADS)

def probabilities(query_block, near_keys, near_weights):
    scores = jnp.einsum('bihd,bjhd->bhij', query_block, near_keys) * (score_scale / (D // HEADS))
    raised = jnp.exp(scores) * near_weights[:, None, None, :]
    return raised / lax.optimization_barrier(jnp.sum(raised, axis=-1, keepdims=True))

def reference(features, cotangent, inner_weight, outer_weight, upward_weight, downward_weight, node_mask, neighbours):
    count = features.shape[0]
    patches = count // PATCH_NODES
    head_size = D // HEADS
    blocks = patches // block_patches
    inputs = features.astype(jnp.float32)
    normed = rms_rows(inputs).astype(jnp.bfloat16)
    projected = jnp.dot(normed, inner_weight, preferred_element_type=jnp.float32)
    raw_queries = projected[:, :D]
    raw_keys = projected[:, D:2 * D]
    queries = head_norm(raw_queries).astype(jnp.bfloat16)
    keys = head_norm(raw_keys).astype(jnp.bfloat16)
    values = projected[:, 2 * D:].astype(jnp.bfloat16)
    key_tiles = keys.reshape(patches, PATCH_NODES, D)
    value_tiles = values.reshape(patches, PATCH_NODES, D)
    weight_tiles = node_mask.astype(jnp.float32)
    query_blocks = queries.reshape(blocks, block_patches, PATCH_NODES, HEADS, head_size)
    index_blocks = neighbours.reshape(blocks, block_patches, NEAR)

    def near_of(index_block):
        near_keys = widen(gather_tiles(index_block, key_tiles))
        near_values = widen(gather_tiles(index_block, value_tiles))
        near_weights = jnp.take(weight_tiles, index_block.reshape(-1), axis=0).reshape(block_patches, NEAR * PATCH_NODES)
        return (near_keys, near_values, near_weights)

    def forward_block(pair):
        query_block, index_block = pair
        near_keys, near_values, near_weights = near_of(index_block)
        probs = probabilities(widen(query_block), near_keys, near_weights)
        mixed = jnp.einsum('bhij,bjhd->bihd', widen(probs.astype(jnp.bfloat16)), near_values)
        return mixed.reshape(block_patches, PATCH_NODES, D).astype(jnp.bfloat16)
    attended = lax.map(forward_block, (query_blocks, index_blocks)).reshape(count, D)
    residual = (inputs + jnp.dot(attended, outer_weight, preferred_element_type=jnp.float32)).astype(jnp.bfloat16)
    middle = residual.astype(jnp.float32)
    second = rms_rows(middle).astype(jnp.bfloat16)
    before = jnp.dot(second, upward_weight, preferred_element_type=jnp.float32)
    hidden = jax.nn.gelu(before).astype(jnp.bfloat16)
    back_hidden = jnp.dot(cotangent, downward_weight.T, preferred_element_type=jnp.float32)
    unused, gelu_back = jax.vjp(jax.nn.gelu, before)
    back_before = gelu_back(back_hidden)[0].astype(jnp.bfloat16)
    grad_down = jnp.dot(hidden.T, cotangent, preferred_element_type=jnp.float32)
    grad_up = jnp.dot(second.T, back_before, preferred_element_type=jnp.float32)
    back_second = jnp.dot(back_before, upward_weight.T, preferred_element_type=jnp.float32)
    unused, middle_back = jax.vjp(rms_rows, middle)
    back_residual = (cotangent.astype(jnp.float32) + middle_back(back_second)[0]).astype(jnp.bfloat16)
    back_attended = jnp.dot(back_residual, outer_weight.T, preferred_element_type=jnp.float32).astype(jnp.bfloat16)
    grad_outer = jnp.dot(attended.T, back_residual, preferred_element_type=jnp.float32)
    back_blocks = back_attended.reshape(blocks, block_patches, PATCH_NODES, HEADS, head_size)

    def backward_block(carry, triple):
        key_sums, value_sums = carry
        query_block, index_block, back_block = triple
        near_keys, near_values, near_weights = near_of(index_block)
        query_wide = widen(query_block)
        probs = probabilities(query_wide, near_keys, near_weights)
        back_out = widen(back_block)
        back_probs = jnp.einsum('bihd,bjhd->bhij', back_out, near_values)
        back_scores = probs * (back_probs - lax.optimization_barrier(jnp.sum(probs * back_probs, axis=-1, keepdims=True))) * (score_scale / head_size)
        scores_low = widen(back_scores.astype(jnp.bfloat16))
        back_queries = jnp.einsum('bhij,bjhd->bihd', scores_low, near_keys).reshape(block_patches * PATCH_NODES, D)
        back_keys = jnp.einsum('bhij,bihd->bjhd', scores_low, query_wide).reshape(block_patches * NEAR, PATCH_NODES, D)
        back_values = jnp.einsum('bhij,bihd->bjhd', widen(probs.astype(jnp.bfloat16)), back_out).reshape(block_patches * NEAR, PATCH_NODES, D)
        flat = index_block.reshape(-1)
        key_sums = key_sums.at[flat].add(back_keys)
        value_sums = value_sums.at[flat].add(back_values)
        return ((key_sums, value_sums), back_queries)
    zeros = jnp.zeros((patches, PATCH_NODES, D), jnp.float32)
    (key_sums, value_sums), back_queries = lax.scan(backward_block, (zeros, zeros), (query_blocks, index_blocks, back_blocks))
    back_queries = back_queries.reshape(count, D)
    unused, query_back = jax.vjp(head_norm, raw_queries)
    unused, key_back = jax.vjp(head_norm, raw_keys)
    back_projected = jnp.concatenate([query_back(back_queries)[0], key_back(key_sums.reshape(count, D))[0], value_sums.reshape(count, D)], axis=-1).astype(jnp.bfloat16)
    grad_inner = jnp.dot(normed.T, back_projected, preferred_element_type=jnp.float32)
    back_normed = jnp.dot(back_projected, inner_weight.T, preferred_element_type=jnp.float32)
    unused, input_back = jax.vjp(rms_rows, inputs)
    back_features = (back_residual.astype(jnp.float32) + input_back(back_normed)[0]).astype(jnp.bfloat16)
    factor = count ** (-0.5)
    return (back_features, grad_inner * factor, grad_outer * factor, grad_up * factor, grad_down * factor)
```

```python
import functools

import jax
import jax.numpy as jnp
from jax import lax
from jax.experimental import pallas as pl
from jax.experimental.pallas import tpu as pltpu
from jax.sharding import PartitionSpec as P

D = 384
HEADS = 8
PATCH_NODES = 128
NEAR = 8


epsilon = 1e-06
score_scale = 5.0


def rms_rows(rows):
    return rows * lax.rsqrt(jnp.mean(rows * rows, axis=-1, keepdims=True) + epsilon)


def head_norm(rows):
    count = rows.shape[0]
    split = rows.reshape(count, HEADS, D // HEADS)
    split = split * lax.rsqrt(jnp.mean(split * split, axis=-1, keepdims=True) + epsilon)
    return split.reshape(count, D)


HEAD = D // HEADS
VALUE_ROW = D
MASK_ROW = 2 * D
WINDOW_ROWS = 2 * D + 16
OFFSETS = (-1, 1, -2, 2)
MESH = pl.DeviceIdType.MESH
VMEM_LIMIT = 40 * 1024 * 1024


def whole():
    return pl.BlockSpec(memory_space=pltpu.VMEM)


def dot(left, right, left_dim, right_dim):
    return lax.dot_general(
        left, right, (((left_dim,), (right_dim,)), ((), ())), preferred_element_type=jnp.float32
    )


def head_major(rows):
    patches = rows.shape[0] // PATCH_NODES
    return rows.reshape(patches, PATCH_NODES, D).transpose(0, 2, 1)


def row_major(tiles):
    return tiles.transpose(0, 2, 1).reshape(tiles.shape[0] * PATCH_NODES, D)


def near_tiles(window_ref, ids, start, size):
    return jnp.concatenate([window_ref[one, start : start + size, :] for one in ids], axis=1)


def weights_of(window_ref, ids):
    return near_tiles(window_ref, ids, MASK_ROW, 16).astype(jnp.float32)[0:1, :]


def softmax(query, key, weights):
    raised = jnp.exp(dot(query, key, 0, 0) * (score_scale / HEAD)) * weights
    return raised * (1.0 / jnp.sum(raised, axis=1, keepdims=True))


def forward_kernel(index_ref, query_ref, window_ref, attended_ref):
    @pl.loop(0, query_ref.shape[0])
    def _(patch):
        ids = [index_ref[patch, slot] for slot in range(NEAR)]
        weights = weights_of(window_ref, ids)
        for head in range(HEADS):
            start = head * HEAD
            key = near_tiles(window_ref, ids, start, HEAD)
            value = near_tiles(window_ref, ids, VALUE_ROW + start, HEAD)
            query = query_ref[patch, start : start + HEAD, :]
            probs = softmax(query, key, weights).astype(jnp.bfloat16)
            attended_ref[patch, start : start + HEAD, :] = dot(value, probs, 1, 1).astype(
                jnp.bfloat16
            )


def backward_kernel(index_ref, query_ref, back_ref, window_ref, back_query_ref, sums_ref):
    sums_ref[...] = jnp.zeros_like(sums_ref)

    @pl.loop(0, query_ref.shape[0])
    def _(patch):
        ids = [index_ref[patch, slot] for slot in range(NEAR)]
        weights = weights_of(window_ref, ids)
        for head in range(HEADS):
            start = head * HEAD
            rows = slice(start, start + HEAD)
            value_rows = slice(VALUE_ROW + start, VALUE_ROW + start + HEAD)
            key = near_tiles(window_ref, ids, start, HEAD)
            value = near_tiles(window_ref, ids, VALUE_ROW + start, HEAD)
            query = query_ref[patch, rows, :]
            back = back_ref[patch, rows, :]
            probs = softmax(query, key, weights)
            weighted = probs * dot(back, value, 0, 0)
            total = jnp.sum(weighted, axis=1, keepdims=True)
            scores = ((weighted - probs * total) * (score_scale / HEAD)).astype(jnp.bfloat16)
            back_query_ref[patch, rows, :] = dot(key, scores, 1, 1)
            back_key = dot(query, scores, 1, 0)
            back_value = dot(back, probs.astype(jnp.bfloat16), 1, 0)
            for slot in range(NEAR):
                columns = slice(slot * PATCH_NODES, (slot + 1) * PATCH_NODES)
                sums_ref[ids[slot], rows, :] += back_key[:, columns]
                sums_ref[ids[slot], value_rows, :] += back_value[:, columns]


def local_call(kernel, out_shape, flops, *operands):
    specs = [pl.BlockSpec(memory_space=pltpu.SMEM)] + [whole()] * (len(operands) - 1)
    return pl.pallas_call(
        kernel,
        out_shape=out_shape,
        in_specs=specs,
        out_specs=jax.tree.map(lambda leaf: whole(), out_shape),
        compiler_params=pltpu.CompilerParams(vmem_limit_bytes=VMEM_LIMIT),
        cost_estimate=pl.CostEstimate(flops=flops, bytes_accessed=8000000, transcendentals=3000000),
    )(*operands)


def inside(cell, count):
    return (cell >= 0) & (cell < count)


def greet(me, count):
    barrier = pltpu.get_barrier_semaphore()
    for step in OFFSETS:

        @pl.when(inside(me + step, count))
        def _():
            pl.semaphore_signal(barrier, inc=1, device_id={"cells": me + step}, device_id_type=MESH)

    pl.semaphore_wait(barrier, jnp.minimum(me, 2) + jnp.minimum(count - 1 - me, 2))


def spread_kernel(count, own_ref, window_ref, send_sem, recv_sem, own_sem):
    me = lax.axis_index("cells")
    own_copy = pltpu.make_async_copy(own_ref, window_ref.at[2], own_sem)
    own_copy.start()
    greet(me, count)
    copies = []
    for place, step in enumerate(OFFSETS):
        copy = pltpu.make_async_remote_copy(
            src_ref=own_ref,
            dst_ref=window_ref.at[2 - step],
            send_sem=send_sem.at[place],
            recv_sem=recv_sem.at[place],
            device_id={"cells": me + step},
            device_id_type=MESH,
        )
        copies.append(copy)
        pl.when(inside(me + step, count))(copy.start)
    own_copy.wait()
    for step, copy in zip(OFFSETS, copies):
        pl.when(inside(me + step, count))(copy.wait_send)
        pl.when(inside(me - step, count))(copy.wait_recv)


def spread(own):
    count = lax.axis_size("cells")
    return pl.pallas_call(
        functools.partial(spread_kernel, count),
        out_shape=jax.ShapeDtypeStruct((5,) + own.shape, own.dtype),
        in_specs=[whole()],
        out_specs=whole(),
        scratch_shapes=[
            pltpu.SemaphoreType.DMA((4,)),
            pltpu.SemaphoreType.DMA((4,)),
            pltpu.SemaphoreType.DMA,
        ],
        compiler_params=pltpu.CompilerParams(
            collective_id=0, has_side_effects=True, vmem_limit_bytes=VMEM_LIMIT
        ),
    )(own)


def collect_kernel(count, sums_ref, own_ref, outgoing, incoming, send_sem, recv_sem):
    me = lax.axis_index("cells")
    for place, step in enumerate(OFFSETS):
        outgoing[place] = sums_ref[2 + step].astype(jnp.bfloat16)
    greet(me, count)
    copies = []
    for place, step in enumerate(OFFSETS):
        copy = pltpu.make_async_remote_copy(
            src_ref=outgoing.at[place],
            dst_ref=incoming.at[place],
            send_sem=send_sem.at[place],
            recv_sem=recv_sem.at[place],
            device_id={"cells": me + step},
            device_id_type=MESH,
        )
        copies.append(copy)
        pl.when(inside(me + step, count))(copy.start)
    own_ref[...] = sums_ref[2]
    for place, (step, copy) in enumerate(zip(OFFSETS, copies)):

        @pl.when(inside(me - step, count))
        def _():
            copy.wait_recv()
            own_ref[...] += incoming[place].astype(jnp.float32)

    for step, copy in zip(OFFSETS, copies):
        pl.when(inside(me + step, count))(copy.wait_send)


def collect(sums):
    count = lax.axis_size("cells")
    slots = (4,) + sums.shape[1:]
    return pl.pallas_call(
        functools.partial(collect_kernel, count),
        out_shape=jax.ShapeDtypeStruct(sums.shape[1:], jnp.float32),
        in_specs=[whole()],
        out_specs=whole(),
        scratch_shapes=[
            pltpu.VMEM(slots, jnp.bfloat16),
            pltpu.VMEM(slots, jnp.bfloat16),
            pltpu.SemaphoreType.DMA((4,)),
            pltpu.SemaphoreType.DMA((4,)),
        ],
        compiler_params=pltpu.CompilerParams(
            collective_id=1, has_side_effects=True, vmem_limit_bytes=VMEM_LIMIT
        ),
    )(sums)


def reversed_bits(number, bits):
    return sum(((number >> bit) & 1) << (bits - 1 - bit) for bit in range(bits))


def halving_kernel(count, factor, term_ref, total_ref, first, later, send_sem, recv_sem):
    me = lax.axis_index("cells")
    bits = count.bit_length() - 1
    sides = [lax.rem(lax.div(me, 2**bit), 2) for bit in range(bits)]
    partners = [me + (1 - 2 * sides[bit]) * 2**bit for bit in range(bits)]
    barrier = pltpu.get_barrier_semaphore()
    for partner in partners:
        pl.semaphore_signal(barrier, inc=1, device_id={"cells": partner}, device_id_type=MESH)
    rows = total_ref.shape[0]
    for block in range(count):
        first[reversed_bits(block, bits)] = term_ref[block * rows : (block + 1) * rows, :].astype(
            jnp.bfloat16
        )
    pl.semaphore_wait(barrier, bits)
    copies = []
    source, base, start = first, 0, 0
    for bit in range(bits):
        half = count >> (bit + 1)
        copy = pltpu.make_async_remote_copy(
            src_ref=source.at[pl.ds(base + (1 - sides[bit]) * half, half)],
            dst_ref=later.at[pl.ds(start, half)],
            send_sem=send_sem.at[bit],
            recv_sem=recv_sem.at[bit],
            device_id={"cells": partners[bit]},
            device_id_type=MESH,
        )
        copy.start()
        copies.append(copy)
        copy.wait_recv()
        for block in range(half):
            mine = source[base + sides[bit] * half + block].astype(jnp.float32)
            added = mine + later[start + block].astype(jnp.float32)
            if bit == bits - 1:
                total_ref[...] = added * factor
            else:
                later[start + block] = added.astype(jnp.bfloat16)
        source, base, start = later, start, start + half
    for copy in copies:
        copy.wait_send()


def halving_scatter(term, factor):
    count = lax.axis_size("cells")
    bits = count.bit_length() - 1
    rows, columns = term.shape[0] // count, term.shape[1]
    return pl.pallas_call(
        functools.partial(halving_kernel, count, factor),
        out_shape=jax.ShapeDtypeStruct((rows, columns), jnp.float32),
        in_specs=[whole()],
        out_specs=whole(),
        scratch_shapes=[
            pltpu.VMEM((count, rows, columns), jnp.bfloat16),
            pltpu.VMEM((count, rows, columns), jnp.bfloat16),
            pltpu.SemaphoreType.DMA((bits,)),
            pltpu.SemaphoreType.DMA((bits,)),
        ],
        compiler_params=pltpu.CompilerParams(
            collective_id=2, has_side_effects=True, vmem_limit_bytes=VMEM_LIMIT
        ),
    )(term)


def per_device(
    features,
    cotangent,
    inner_weight,
    outer_weight,
    upward_weight,
    downward_weight,
    node_mask,
    neighbours,
):
    count = features.shape[0]
    patches = count // PATCH_NODES
    cells = lax.axis_size("cells")
    factor = (cells * count) ** (-0.5)
    position = lax.axis_index("cells")
    inputs = features.astype(jnp.float32)
    normed = rms_rows(inputs).astype(jnp.bfloat16)
    projected = jnp.dot(normed, inner_weight, preferred_element_type=jnp.float32)
    raw_queries = projected[:, :D]
    raw_keys = projected[:, D : 2 * D]
    queries = head_norm(raw_queries).astype(jnp.bfloat16)
    keys = head_norm(raw_keys).astype(jnp.bfloat16)
    values = projected[:, 2 * D :].astype(jnp.bfloat16)
    own = jnp.concatenate(
        [
            head_major(keys),
            head_major(values),
            jnp.broadcast_to(
                node_mask.astype(jnp.bfloat16)[:, None, :], (patches, 16, PATCH_NODES)
            ),
        ],
        axis=1,
    )
    window = spread(own).reshape(5 * patches, WINDOW_ROWS, PATCH_NODES)
    local_index = neighbours - (position - 2) * patches
    query_tiles = head_major(queries)
    products = 2 * patches * NEAR * PATCH_NODES * PATCH_NODES * D
    attended = row_major(
        local_call(
            forward_kernel,
            jax.ShapeDtypeStruct((patches, D, PATCH_NODES), jnp.bfloat16),
            2 * products,
            local_index,
            query_tiles,
            window,
        )
    )
    residual = (
        inputs + jnp.dot(attended, outer_weight, preferred_element_type=jnp.float32)
    ).astype(jnp.bfloat16)
    middle = residual.astype(jnp.float32)
    second = rms_rows(middle).astype(jnp.bfloat16)
    before = jnp.dot(second, upward_weight, preferred_element_type=jnp.float32)
    hidden = jax.nn.gelu(before).astype(jnp.bfloat16)
    back_hidden = jnp.dot(cotangent, downward_weight.T, preferred_element_type=jnp.float32)
    unused, gelu_back = jax.vjp(jax.nn.gelu, before)
    back_before = gelu_back(back_hidden)[0].astype(jnp.bfloat16)
    term_down = jnp.dot(hidden.T, cotangent, preferred_element_type=jnp.float32)
    term_up = jnp.dot(second.T, back_before, preferred_element_type=jnp.float32)
    back_second = jnp.dot(back_before, upward_weight.T, preferred_element_type=jnp.float32)
    unused, middle_back = jax.vjp(rms_rows, middle)
    back_residual = (cotangent.astype(jnp.float32) + middle_back(back_second)[0]).astype(
        jnp.bfloat16
    )
    back_attended = jnp.dot(
        back_residual, outer_weight.T, preferred_element_type=jnp.float32
    ).astype(jnp.bfloat16)
    term_outer = jnp.dot(attended.T, back_residual, preferred_element_type=jnp.float32)
    early = jnp.concatenate(
        [
            term_outer.reshape(cells, -1, D),
            term_up.reshape(cells, D // cells, -1, D).transpose(0, 2, 1, 3).reshape(cells, -1, D),
            term_down.reshape(cells, -1, D),
        ],
        axis=1,
    )
    summed = lax.psum_scatter(early, "cells", scatter_dimension=0, tiled=False) * factor
    back_query_tiles, sums = local_call(
        backward_kernel,
        (
            jax.ShapeDtypeStruct((patches, D, PATCH_NODES), jnp.float32),
            jax.ShapeDtypeStruct((5 * patches, 2 * D, PATCH_NODES), jnp.float32),
        ),
        5 * products,
        local_index,
        query_tiles,
        head_major(back_attended),
        window,
    )
    back_queries = row_major(back_query_tiles)
    collected = collect(sums.reshape(5, patches, 2 * D, PATCH_NODES))
    own_keys = row_major(collected[:, :D])
    own_values = row_major(collected[:, D:])
    unused, query_back = jax.vjp(head_norm, raw_queries)
    unused, key_back = jax.vjp(head_norm, raw_keys)
    back_projected = jnp.concatenate(
        [query_back(back_queries)[0], key_back(own_keys)[0], own_values],
        axis=-1,
    ).astype(jnp.bfloat16)
    term_inner = jnp.dot(normed.T, back_projected, preferred_element_type=jnp.float32)
    back_normed = jnp.dot(back_projected, inner_weight.T, preferred_element_type=jnp.float32)
    unused, input_back = jax.vjp(rms_rows, inputs)
    back_features = (back_residual.astype(jnp.float32) + input_back(back_normed)[0]).astype(
        jnp.bfloat16
    )
    rows = D // cells
    outer_rows, up_rows = rows, rows * (term_up.shape[1] // D)
    summed_up = summed[outer_rows : outer_rows + up_rows].reshape(-1, rows, D)
    return (
        back_features,
        halving_scatter(term_inner, factor),
        summed[:outer_rows],
        summed_up.transpose(1, 0, 2).reshape(rows, -1),
        summed[outer_rows + up_rows :],
    )


def solution(mesh):
    placed = (
        P(("groups", "cells"), None),
        P(("groups", "cells"), None),
        P(),
        P(),
        P(),
        P(),
        P(("groups", "cells"), None),
        P(("groups", "cells"), None),
    )
    return jax.shard_map(
        per_device,
        mesh=mesh,
        in_specs=placed,
        out_specs=(
            P(("groups", "cells"), None),
            P(("groups", "cells"), None),
            P(("groups", "cells"), None),
            P(("groups", "cells"), None),
            P(("groups", "cells"), None),
        ),
        check_vma=False,
    )
```
